32 devices in a mesh: phonon: 2 (over x), beam: 8 (over z, y), sub: 2 (over core).
Axes of the slice: x: 2, y: 2, z: 4, core: 2. Of those that a mesh axis runs over, the one named last changes fastest.
Arguments:
- atom_species: int32 [4, 2048], P('phonon'), parts along dimension 0, may hold values from 0 to 3
- atom_cells: int32 [2, 4, 2048], P(None, 'phonon'), parts along dimension 1, may hold values from 0 to 511
- profiles: bfloat16 [4, 512], replicated, may hold values from -6 to 6
- beam_freqs: int32 [2, 32], P(None, ('beam', 'sub')), may hold values from -32 to 30, as said below
- amplitude: float32 [32], P(('beam', 'sub')), may hold values from 0.5 to 2
- aberration: float32 [32], P(('beam', 'sub')), may hold values from -3.140625 to 3.140625
- probes: int32 [2, 64], replicated, may hold values from 0 to 255
Outputs:
- intensity: float32 [128, 256, 256], P('phonon', ('beam', 'sub')), parts along dimension 0
The draws below stay inside these ranges and needn't reach their ends.
There are 2 independent parts, one for each index of `phonon`. The reference program is written for one: setup_inputs(seed, part) draws one part's arguments, and reference() takes and returns one part's arrays. A program takes and returns all parts, laid end to end along the dimension named above; an argument that names none is the same for every part. Nothing has to cross between parts.
Inputs may be any that keep to these rules, and one draw needn't show every extreme that they name: `beam_freqs`: every column is a pair of even frequencies; no pair repeats.
All inputs are finite; a program needn't handle non-finite values.
Results may differ from the reference program's by a relative error of at most 0.015.
Values may be sent and summed in bfloat16 or wider, within the bound.
A program may use at most 64 MiB of HBM per device.

```python
import math
import jax
import jax.numpy as jnp
from jax import lax

NPIX = 512
NOUT = 256
NSPEC = 4
SLICES = 2
ATOMS = 2048
BEAMS = 32
PROBES = 64


def draw_beam_freqs(key, part):
    side_count = 32
    inner = 1 + jax.random.permutation(jax.random.fold_in(key, 11), side_count * side_count - 2)[:BEAMS - 2]
    chosen = jnp.concatenate([jnp.array([0, side_count * side_count - 1], dtype=jnp.int32), inner.astype(jnp.int32)])
    chosen = jax.random.permutation(jax.random.fold_in(key, 12), chosen)
    first_freq = 2 * (chosen // side_count - side_count // 2)
    second_freq = 2 * (chosen % side_count - side_count // 2)
    return jnp.stack([first_freq, second_freq]).astype(jnp.int32)


def with_ends(values, rng, smallest, top_value):
    longest = values.shape.index(max(values.shape))
    spots = []
    for shift in (0, 1):
        where = [jax.random.randint(jax.random.fold_in(rng, axis), (), 0, length) for axis, length in enumerate(values.shape)]
        where[longest] = (where[longest] + shift) % values.shape[longest]
        spots.append(tuple(where))
    return values.at[spots[0]].set(smallest).at[spots[1]].set(top_value)


def steps_of(key, extent, shards, least, largest):
    loudness, own = 1.0, jax.random.fold_in(key, 6)
    for dim, parts in shards:
        steps = jnp.exp(jax.random.uniform(jax.random.fold_in(own, dim), (parts,), jnp.float32, least / len(shards), largest / len(shards)))
        loudness = loudness * jnp.repeat(steps, extent[dim] // parts).reshape([-1 if axis == dim else 1 for axis in range(len(extent))])
    return loudness


def gaussian(key, extent, width, bound, kind=jnp.bfloat16):
    values = jax.random.normal(key, extent, jnp.float32) * width
    return jnp.minimum(jnp.maximum(values, -bound), bound).astype(kind)


def setup_inputs(seed: int = 0, part: int = 0) -> dict:
    splits = jax.random.split(jax.random.key(seed), 8)
    part_keys = jax.random.split(jax.random.fold_in(splits[7], part), 8)
    atom_species = with_ends(jax.random.randint(part_keys[0], (SLICES, ATOMS), 0, NSPEC), jax.random.fold_in(part_keys[0], 1), 0, NSPEC - 1).astype(jnp.int32)
    atom_cells = with_ends(jax.random.randint(part_keys[1], (2, SLICES, ATOMS), 0, NPIX), jax.random.fold_in(part_keys[1], 1), 0, NPIX - 1).astype(jnp.int32)
    profiles = gaussian(splits[2], (NSPEC, NPIX), 1.0, 6.0)
    beam_freqs = draw_beam_freqs(jax.random.fold_in(splits[7], 71), part)
    amplitude = jnp.clip(jnp.exp(math.log(2.0) - 1.3862944 * jax.random.uniform(splits[4], (BEAMS,), jnp.float32) ** steps_of(splits[4], (BEAMS,), ((0, 16),), -0.2, 0.2)), 0.5, 2.0)
    aberration = jnp.clip(jax.random.uniform(splits[5], (BEAMS,), jnp.float32, -3.140625, 3.140625), -3.140625, 3.140625)
    probes = with_ends(jax.random.randint(splits[6], (2, PROBES), 0, NOUT), jax.random.fold_in(splits[6], 1), 0, NOUT - 1).astype(jnp.int32)
    return dict(atom_species=atom_species, atom_cells=atom_cells, profiles=profiles, beam_freqs=beam_freqs, amplitude=amplitude, aberration=aberration, probes=probes)


def to_half(values):
    return lax.optimization_barrier(values.astype(jnp.bfloat16))

def signed_freqs(length):
    positions = jnp.arange(length, dtype=jnp.int32)
    return jnp.where(positions < length // 2, positions, positions - length)

def phase_table(rows_in, cols_in, modulus, direction):
    product = jnp.mod(rows_in[:, None] * cols_in[None, :], modulus)
    turn_angle = direction * 2.0 * math.pi / modulus * product.astype(jnp.float32)
    return (jnp.cos(turn_angle).astype(jnp.bfloat16), jnp.sin(turn_angle).astype(jnp.bfloat16))

def propagator(signed_list, points):
    square = signed_list * signed_list
    summed = square[:, None] + square[None, :]
    turn_angle = -math.pi / points * jnp.mod(summed, 2 * points).astype(jnp.float32)
    window = jnp.where(9 * summed < points * points, 1.0 / (points * points), 0.0).astype(jnp.float32)
    return (jnp.cos(turn_angle) * window, jnp.sin(turn_angle) * window)

def profile_rows(species, offsets, profiles, points):
    columns = jnp.arange(points, dtype=jnp.int32)
    where_at = species[:, None] * points + jnp.mod(columns[None, :] - offsets[:, None], points)
    return jnp.take(profiles.reshape(-1), where_at, axis=0)

def potential(species, x_cells, y_cells, profiles, points):
    rows_x = profile_rows(species, x_cells, profiles, points)
    rows_y = profile_rows(species, y_cells, profiles, points)
    return lax.dot_general(rows_x, rows_y, (((0,), (0,)), ((), ())), preferred_element_type=jnp.float32)

def matmul(left_op, right_op):
    return jnp.dot(left_op.astype(jnp.float32), right_op.astype(jnp.float32), precision=lax.Precision.HIGHEST)

def from_left(pair_table, wave_real, wave_imag):
    cosine_part, sine_part = pair_table
    return (matmul(cosine_part, wave_real) - matmul(sine_part, wave_imag), matmul(cosine_part, wave_imag) + matmul(sine_part, wave_real))

def from_right(pair_table, wave_real, wave_imag):
    cosine_part, sine_part = pair_table
    return (matmul(wave_real, cosine_part.T) - matmul(wave_imag, sine_part.T), matmul(wave_imag, cosine_part.T) + matmul(wave_real, sine_part.T))

def one_slice(wave_real, wave_imag, transmit, forward, inverse, spread):
    trans_real, trans_imag = transmit
    mixed_re = to_half(wave_real * trans_real - wave_imag * trans_imag)
    mixed_im = to_half(wave_real * trans_imag + wave_imag * trans_real)
    half_re, half_im = from_left(forward, mixed_re, mixed_im)
    half_re, half_im = (to_half(half_re), to_half(half_im))
    spec_re, spec_im = from_right(forward, half_re, half_im)
    prop_real, prop_imag = spread
    shaped_re = to_half(spec_re * prop_real - spec_im * prop_imag)
    shaped_im = to_half(spec_re * prop_imag + spec_im * prop_real)
    back_re, back_im = from_left(inverse, shaped_re, shaped_im)
    back_re, back_im = (to_half(back_re), to_half(back_im))
    return from_right(inverse, back_re, back_im)

def probe_weights(beam_freqs, amplitude, aberration, probes, coarse):
    length = beam_freqs.shape[1]
    probe_shift = jnp.mod(probes[0][:, None] * beam_freqs[0][None, :] + probes[1][:, None] * beam_freqs[1][None, :], coarse)
    turn_angle = 2.0 * math.pi / coarse * probe_shift.astype(jnp.float32) + aberration[None, :]
    weight = amplitude[None, :] * (1.0 / math.sqrt(length))
    return (to_half(weight * jnp.cos(turn_angle)), to_half(-(weight * jnp.sin(turn_angle))))

def reference(atom_species, atom_cells, profiles, beam_freqs, amplitude, aberration, probes):
    transmits = []
    for layer_index in range(SLICES):
        field = potential(atom_species[layer_index], atom_cells[0, layer_index], atom_cells[1, layer_index], profiles, NPIX)
        slice_phase = field * (1.5 / math.sqrt(ATOMS))
        transmits.append((jnp.cos(slice_phase), jnp.sin(slice_phase)))
    positions = jnp.arange(NPIX, dtype=jnp.int32)
    kept_freqs = signed_freqs(NOUT)
    coarse = jnp.arange(NOUT, dtype=jnp.int32)
    forward_full = phase_table(positions, positions, NPIX, -1.0)
    inverse_full = phase_table(positions, positions, NPIX, 1.0)
    forward_crop = phase_table(kept_freqs, positions, NPIX, -1.0)
    inverse_crop = phase_table(coarse, coarse, NOUT, 1.0)
    prop_full = propagator(signed_freqs(NPIX), NPIX)
    prop_crop = propagator(kept_freqs, NPIX)

    def one_beam(wave_freq):
        start_phase = jnp.mod(wave_freq[0] * positions[:, None] + wave_freq[1] * positions[None, :], NPIX)
        start_angle = 2.0 * math.pi / NPIX * start_phase.astype(jnp.float32)
        wave_real, wave_imag = (jnp.cos(start_angle), jnp.sin(start_angle))
        for layer_index in range(SLICES):
            if layer_index == SLICES - 1:
                wave_real, wave_imag = one_slice(wave_real, wave_imag, transmits[layer_index], forward_crop, inverse_crop, prop_crop)
            else:
                wave_real, wave_imag = one_slice(wave_real, wave_imag, transmits[layer_index], forward_full, inverse_full, prop_full)
        return to_half(jnp.stack([wave_real, wave_imag]))
    beam_waves = lax.map(one_beam, beam_freqs.T)
    coef_real, coef_imag = probe_weights(beam_freqs, amplitude, aberration, probes, NOUT)
    flat_real = beam_waves[:, 0].reshape(BEAMS, NOUT * NOUT)
    flat_imag = beam_waves[:, 1].reshape(BEAMS, NOUT * NOUT)
    psi_real = matmul(coef_real, flat_real) - matmul(coef_imag, flat_imag)
    psi_imag = matmul(coef_real, flat_imag) + matmul(coef_imag, flat_real)
    return (psi_real * psi_real + psi_imag * psi_imag).reshape(PROBES, NOUT, NOUT)
```

```python
import functools
import math

import jax
import jax.numpy as jnp
import ml_dtypes
import numpy as np
from jax import lax
from jax.experimental import pallas as pl
from jax.experimental.pallas import tpu as pltpu
from jax.sharding import PartitionSpec as P

NOUT = 256
LOW = 64
BF = jnp.bfloat16
F32 = jnp.float32


def fit_turn_polys():
    nodes = np.cos(np.pi * (np.arange(400) + 0.5) / 400)
    squares = (nodes + 1.0) * 0.125
    turns = np.sqrt(squares)
    cosine = np.polynomial.chebyshev.Chebyshev.fit(
        squares, np.cos(2 * np.pi * turns), 6, domain=[0, 0.25]
    )
    sine = np.polynomial.chebyshev.Chebyshev.fit(
        squares, np.sin(2 * np.pi * turns) / turns, 6, domain=[0, 0.25]
    )
    to_list = lambda fit: [float(c) for c in fit.convert(kind=np.polynomial.Polynomial).coef]
    return to_list(cosine), to_list(sine)


COS_POLY, SIN_POLY = fit_turn_polys()


def cos_sin_turns(turns):
    rest = turns - jnp.round(turns)
    square = rest * rest
    cosine = jnp.full_like(square, COS_POLY[-1])
    for c in COS_POLY[-2::-1]:
        cosine = cosine * square + c
    sine = jnp.full_like(square, SIN_POLY[-1])
    for c in SIN_POLY[-2::-1]:
        sine = sine * square + c
    return cosine, sine * rest


def window_freqs(points):
    half = NOUT // 2
    reach = math.isqrt((points * points - 1) // 9)
    side = max(reach + 1, half)
    side = min(-(-side // 64) * 64, points // 2)
    return np.concatenate(
        [np.arange(-half, half), np.arange(half, side), np.arange(-side, -half)]
    ).astype(np.int64)


def table_parts(rows, cols, modulus, sign):
    angle = sign * 2.0 * np.pi / modulus * np.mod(rows[:, None] * cols[None, :], modulus)
    return np.cos(angle), np.sin(angle)


def left_table(real, imag):
    return np.block([[real, -imag], [imag, real]]).astype(ml_dtypes.bfloat16)


def right_table(real, imag):
    return np.block([[real, imag], [-imag, real]]).astype(ml_dtypes.bfloat16)


def propagator_parts(freqs, points):
    q = freqs[:, None] ** 2 + freqs[None, :] ** 2
    angle = -np.pi / points * np.mod(q, 2 * points)
    window = np.where(9 * q < points * points, 1.0 / (points * points), 0.0)
    return np.stack([np.cos(angle) * window, np.sin(angle) * window]).astype(np.float32)


def dot(a, b):
    return jnp.dot(a, b, preferred_element_type=F32)


def wave_kernel(
    total_beams,
    freqs_ref,
    amp_ref,
    aber_ref,
    species_ref,
    cells_ref,
    prof_ref,
    probes_ref,
    lf_ref,
    rf_ref,
    lg_ref,
    rg_ref,
    lfc_ref,
    rfc_ref,
    lgc_ref,
    rgc_ref,
    pf_ref,
    out_ref,
    coef_ref,
    field_ref,
    rows_ref,
    tall_ref,
    wide_ref,
    tall_c,
    wide_c,
):
    kinds, points = prof_ref.shape
    slices, atoms = species_ref.shape
    beams = out_ref.shape[0]
    window = pf_ref.shape[1]

    stacked = []
    for s in range(kinds):
        row = jnp.broadcast_to(prof_ref[s : s + 1, :].astype(F32), (LOW, points))
        stacked.append(pltpu.roll(row, 0, 1, stride=1, stride_axis=0))
    tab = jnp.transpose(jnp.concatenate(stacked, axis=0)).astype(BF)

    scale = 1.5 / math.sqrt(atoms) / (2.0 * math.pi)
    chunk = min(512, atoms)
    slot = lax.broadcasted_iota(jnp.int32, (kinds * LOW, chunk), 0)
    for layer in range(slices):
        for axis in range(2):
            for first in range(0, atoms, chunk):
                here = slice(first, first + chunk)
                cell = cells_ref[axis, layer : layer + 1, here]
                key = species_ref[layer : layer + 1, here] * LOW + jnp.bitwise_and(cell, LOW - 1)
                picked = (slot == key).astype(F32).astype(BF)
                rows = dot(tab, picked)
                amount = LOW
                while amount < points:
                    moved = jnp.concatenate([rows[points - amount :], rows[: points - amount]], 0)
                    rows = jnp.where(jnp.bitwise_and(cell, amount) != 0, moved, rows)
                    amount *= 2
                rows_ref[axis, :, here] = rows.astype(BF)
        field = lax.dot_general(
            rows_ref[0], rows_ref[1], (((1,), (1,)), ((), ())), preferred_element_type=F32
        )
        cosine, sine = cos_sin_turns(field * scale)
        field_ref[2 * layer] = cosine
        field_ref[2 * layer + 1] = sine

    down = lax.broadcasted_iota(jnp.int32, (points, 1), 0)
    along = lax.broadcasted_iota(jnp.int32, (1, points), 1)
    for b in range(beams):
        fx, fy = freqs_ref[0, b], freqs_ref[1, b]
        col_re, col_im = cos_sin_turns(
            jnp.bitwise_and(down * fx, points - 1).astype(F32) * (1.0 / points)
        )
        row_re, row_im = cos_sin_turns(
            jnp.bitwise_and(along * fy, points - 1).astype(F32) * (1.0 / points)
        )
        wave_re = col_re * row_re - col_im * row_im
        wave_im = col_re * row_im + col_im * row_re
        for layer in range(slices):
            tr, ti = field_ref[2 * layer], field_ref[2 * layer + 1]
            tall_ref[:points] = (wave_re * tr - wave_im * ti).astype(BF)
            tall_ref[points:] = (wave_re * ti + wave_im * tr).astype(BF)
            last = layer == slices - 1
            n = NOUT if last else window
            lf, rf = (lfc_ref, rfc_ref) if last else (lf_ref, rf_ref)
            lg, rg = (lgc_ref, rgc_ref) if last else (lg_ref, rg_ref)
            width = rg.shape[1] // 2
            wide_ref[:n, :points] = dot(lf[:n], tall_ref[...]).astype(BF)
            wide_ref[:n, points:] = dot(lf[n:], tall_ref[...]).astype(BF)
            half = wide_ref[:n]
            sr = dot(half, rf[:, :n])
            si = dot(half, rf[:, n:])
            pr, pi = pf_ref[0, :n, :n], pf_ref[1, :n, :n]
            tall_c[:n, :n] = (sr * pr - si * pi).astype(BF)
            tall_c[n : 2 * n, :n] = (sr * pi + si * pr).astype(BF)
            shaped = tall_c[: 2 * n, :n]
            wide_c[:width, :n] = dot(lg[:width], shaped).astype(BF)
            wide_c[:width, n : 2 * n] = dot(lg[width:], shaped).astype(BF)
            back = wide_c[:width, : 2 * n]
            wave_re = dot(back, rg[:, :width])
            wave_im = dot(back, rg[:, width:])
        out_ref[b, 0] = wave_re.astype(BF)
        out_ref[b, 1] = wave_im.astype(BF)
        place = probes_ref[0:1, :] * fx + probes_ref[1:2, :] * fy
        turns = jnp.bitwise_and(place, NOUT - 1).astype(F32) * (1.0 / NOUT)
        cosine, sine = cos_sin_turns(turns + aber_ref[b] * (0.5 / math.pi))
        weight = amp_ref[b] * (1.0 / math.sqrt(total_beams))
        coef_ref[b, 0:1, :] = weight * cosine
        coef_ref[b, 1:2, :] = -(weight * sine)


def local_waves(species, cells, profiles, freqs, amplitude, aberration, probes, total_beams):
    points = profiles.shape[1]
    beams = freqs.shape[1]
    atoms = species.shape[1]
    kept = window_freqs(points)
    window = len(kept)
    grid = np.arange(points)
    coarse = np.arange(NOUT)
    crop = kept[:NOUT]
    fr, fi = table_parts(kept, grid, points, -1.0)
    cr, ci = fr[:NOUT], fi[:NOUT]
    gr, gi = table_parts(coarse, crop, NOUT, 1.0)
    tables = [
        left_table(fr, fi),
        right_table(fr.T, fi.T),
        left_table(fr.T, -fi.T),
        right_table(fr, -fi),
        left_table(cr, ci),
        right_table(cr.T, ci.T),
        left_table(gr, gi),
        right_table(gr.T, gi.T),
        propagator_parts(kept, points),
    ]
    vmem = pl.BlockSpec(memory_space=pltpu.VMEM)
    smem = pl.BlockSpec(memory_space=pltpu.SMEM)
    return pl.pallas_call(
        functools.partial(wave_kernel, total_beams),
        out_shape=(
            jax.ShapeDtypeStruct((beams, 2, NOUT, NOUT), BF),
            jax.ShapeDtypeStruct((beams, 2, probes.shape[1]), F32),
        ),
        in_specs=[smem] * 3 + [vmem] * (4 + len(tables)),
        out_specs=(vmem, vmem),
        scratch_shapes=[
            pltpu.VMEM((2 * species.shape[0], points, points), F32),
            pltpu.VMEM((2, points, atoms), BF),
            pltpu.VMEM((2 * points, points), BF),
            pltpu.VMEM((window, 2 * points), BF),
            pltpu.VMEM((2 * window, window), BF),
            pltpu.VMEM((points, 2 * window), BF),
        ],
        compiler_params=pltpu.CompilerParams(vmem_limit_bytes=56 * 1024 * 1024),
    )(freqs, amplitude, aberration, species, cells, profiles, probes, *map(jnp.asarray, tables))


def shards(atom_species, atom_cells, profiles, beam_freqs, amplitude, aberration, probes):
    groups = lax.axis_size("beam") * lax.axis_size("sub")
    beams = beam_freqs.shape[1]
    count = probes.shape[1]
    waves, coefs = local_waves(
        atom_species, atom_cells, profiles, beam_freqs, amplitude, aberration, probes, beams * groups
    )
    rows = NOUT // groups
    waves = waves.reshape(beams, 2, groups, rows, NOUT)
    coefs = jnp.pad(coefs.astype(BF), ((0, 0), (0, 0), (0, NOUT - count)))
    coefs = jnp.broadcast_to(coefs[:, :, None, None, :], (beams, 2, groups, 1, NOUT))
    sent = jnp.concatenate([waves, coefs], axis=3)
    got = lax.all_to_all(sent, ("beam", "sub"), split_axis=2, concat_axis=0, tiled=True)
    got = got[:, :, 0]
    coef = got[:, :, rows, :count]
    coef_re, coef_im = coef[:, 0], coef[:, 1]
    flat = got[:, :, :rows].reshape(beams * groups * 2, rows * NOUT)
    left_re = jnp.stack([coef_re, -coef_im], axis=1).reshape(beams * groups * 2, count)
    left_im = jnp.stack([coef_im, coef_re], axis=1).reshape(beams * groups * 2, count)
    over = (((0,), (0,)), ((), ()))
    psi_re = lax.dot_general(left_re, flat, over, preferred_element_type=F32)
    psi_im = lax.dot_general(left_im, flat, over, preferred_element_type=F32)
    return (psi_re * psi_re + psi_im * psi_im).reshape(count, rows, NOUT)


def solution(mesh):
    return jax.shard_map(
        shards,
        mesh=mesh,
        in_specs=(
            P("phonon", None),
            P(None, "phonon", None),
            P(),
            P(None, ("beam", "sub")),
            P(("beam", "sub")),
            P(("beam", "sub")),
            P(),
        ),
        out_specs=P("phonon", ("beam", "sub"), None),
        check_vma=False,
    )
```

```python
import functools
import math

import jax
import jax.numpy as jnp
import ml_dtypes
import numpy as np
from jax import lax
from jax.experimental import pallas as pl
from jax.experimental.pallas import tpu as pltpu
from jax.sharding import PartitionSpec as P

NOUT = 256
LOW = 64
BF = jnp.bfloat16
F32 = jnp.float32


def fit_turn_polys():
    nodes = np.cos(np.pi * (np.arange(400) + 0.5) / 400)
    squares = (nodes + 1.0) * 0.125
    turns = np.sqrt(squares)
    cosine = np.polynomial.chebyshev.Chebyshev.fit(
        squares, np.cos(2 * np.pi * turns), 6, domain=[0, 0.25]
    )
    sine = np.polynomial.chebyshev.Chebyshev.fit(
        squares, np.sin(2 * np.pi * turns) / turns, 6, domain=[0, 0.25]
    )
    to_list = lambda fit: [float(c) for c in fit.convert(kind=np.polynomial.Polynomial).coef]
    return to_list(cosine), to_list(sine)


COS_POLY, SIN_POLY = fit_turn_polys()


def cos_sin_turns(turns):
    rest = turns - jnp.round(turns)
    square = rest * rest
    cosine = jnp.full_like(square, COS_POLY[-1])
    for c in COS_POLY[-2::-1]:
        cosine = cosine * square + c
    sine = jnp.full_like(square, SIN_POLY[-1])
    for c in SIN_POLY[-2::-1]:
        sine = sine * square + c
    return cosine, sine * rest


def window_freqs(points):
    half = NOUT // 2
    reach = math.isqrt((points * points - 1) // 9)
    side = max(reach + 1, half)
    side = min(-(-side // 64) * 64, points // 2)
    return np.concatenate(
        [np.arange(-half, half), np.arange(half, side), np.arange(-side, -half)]
    ).astype(np.int64)


def table_parts(rows, cols, modulus, sign):
    angle = sign * 2.0 * np.pi / modulus * np.mod(rows[:, None] * cols[None, :], modulus)
    return np.cos(angle), np.sin(angle)


def left_table(real, imag):
    return np.block([[real, -imag], [imag, real]]).astype(ml_dtypes.bfloat16)


def right_table(real, imag):
    return np.block([[real, imag], [-imag, real]]).astype(ml_dtypes.bfloat16)


def propagator_parts(freqs, points):
    q = freqs[:, None] ** 2 + freqs[None, :] ** 2
    angle = -np.pi / points * np.mod(q, 2 * points)
    window = np.where(9 * q < points * points, 1.0 / (points * points), 0.0)
    return np.stack([np.cos(angle) * window, np.sin(angle) * window]).astype(np.float32)


def dot(a, b):
    return jnp.dot(a, b, preferred_element_type=F32)


def wave_kernel(
    total_beams,
    freqs_ref,
    amp_ref,
    aber_ref,
    species_ref,
    cells_ref,
    prof_ref,
    probes_ref,
    lf_ref,
    rf_ref,
    lgc_ref,
    rgc_ref,
    pf_ref,
    out_ref,
    field_ref,
    rows_ref,
    tall_ref,
    wide_ref,
    tall_c,
    wide_c,
):
    kinds, points = prof_ref.shape
    slices, atoms = species_ref.shape
    beams = freqs_ref.shape[1]
    groups = out_ref.shape[0]
    size = NOUT // groups
    window = pf_ref.shape[1]

    stacked = []
    for s in range(kinds):
        row = jnp.broadcast_to(prof_ref[s : s + 1, :].astype(F32), (LOW, points))
        stacked.append(pltpu.roll(row, 0, 1, stride=1, stride_axis=0))
    tab = jnp.transpose(jnp.concatenate(stacked, axis=0)).astype(BF)

    scale = 1.5 / math.sqrt(atoms) / (2.0 * math.pi)
    chunk = min(512, atoms)
    slot = lax.broadcasted_iota(jnp.int32, (kinds * LOW, chunk), 0)
    for layer in range(slices):
        for axis in range(2):
            for first in range(0, atoms, chunk):
                here = slice(first, first + chunk)
                cell = cells_ref[axis, layer : layer + 1, here]
                key = species_ref[layer : layer + 1, here] * LOW + jnp.bitwise_and(cell, LOW - 1)
                picked = (slot == key).astype(F32).astype(BF)
                rows = dot(tab, picked)
                amount = LOW
                while amount < points:
                    moved = jnp.concatenate([rows[points - amount :], rows[: points - amount]], 0)
                    rows = jnp.where(jnp.bitwise_and(cell, amount) != 0, moved, rows)
                    amount *= 2
                rows_ref[axis, :, here] = rows.astype(BF)
        field = lax.dot_general(
            rows_ref[0], rows_ref[1], (((1,), (1,)), ((), ())), preferred_element_type=F32
        )
        cosine, sine = cos_sin_turns(field * scale)
        field_ref[2 * layer] = cosine
        field_ref[2 * layer + 1] = sine

    down = lax.broadcasted_iota(jnp.int32, (points, 1), 0)
    along = lax.broadcasted_iota(jnp.int32, (1, points), 1)
    coef_rows = []
    for b in range(beams):
        fx, fy = freqs_ref[0, b], freqs_ref[1, b]
        col_re, col_im = cos_sin_turns(
            jnp.bitwise_and(down * fx, points - 1).astype(F32) * (1.0 / points)
        )
        row_re, row_im = cos_sin_turns(
            jnp.bitwise_and(along * fy, points - 1).astype(F32) * (1.0 / points)
        )
        wave_re = col_re * row_re - col_im * row_im
        wave_im = col_re * row_im + col_im * row_re
        for layer in range(slices):
            tr, ti = field_ref[2 * layer], field_ref[2 * layer + 1]
            tall_ref[:points] = (wave_re * tr - wave_im * ti).astype(BF)
            tall_ref[points:] = (wave_re * ti + wave_im * tr).astype(BF)
            last = layer == slices - 1
            n = NOUT if last else window
            lg, rg = (lgc_ref, rgc_ref) if last else (rf_ref, lf_ref)
            width = rg.shape[1] // 2
            wide_ref[:n, :points] = dot(lf_ref[:n], tall_ref[...]).astype(BF)
            wide_ref[:n, points:] = dot(lf_ref[window : window + n], tall_ref[...]).astype(BF)
            half = wide_ref[:n]
            sr = dot(half, rf_ref[:, :n])
            si = dot(half, rf_ref[:, window : window + n])
            pr, pi = pf_ref[0, :n, :n], pf_ref[1, :n, :n]
            tall_c[:n, :n] = (sr * pr - si * pi).astype(BF)
            tall_c[n : 2 * n, :n] = (sr * pi + si * pr).astype(BF)
            shaped = tall_c[: 2 * n, :n]
            wide_c[:width, :n] = dot(lg[:width], shaped).astype(BF)
            wide_c[:width, n : 2 * n] = dot(lg[width:], shaped).astype(BF)
            back = wide_c[:width, : 2 * n]
            wave_re = dot(back, rg[:, :width])
            wave_im = dot(back, rg[:, width:])
        for part, wave in enumerate((wave_re, wave_im)):
            start = (2 * b + part) * size
            if size % 16 == 0:
                for g in range(groups):
                    out_ref[g, start : start + size] = wave[g * size : (g + 1) * size].astype(BF)
            else:
                blocks = wave.reshape(groups, size, NOUT).astype(BF)
                out_ref[:, start : start + size] = blocks
        place = probes_ref[0:1, :] * fx + probes_ref[1:2, :] * fy
        turns = jnp.bitwise_and(place, NOUT - 1).astype(F32) * (1.0 / NOUT)
        cosine, sine = cos_sin_turns(turns + aber_ref[b] * (0.5 / math.pi))
        weight = amp_ref[b] * (1.0 / math.sqrt(total_beams))
        coef_rows += [weight * cosine, -(weight * sine)]
    count = probes_ref.shape[1]
    coefs = jnp.concatenate(coef_rows, axis=0)
    coefs = jnp.pad(coefs, ((0, 16 - 2 * beams), (0, NOUT - count))).astype(BF)
    for g in range(groups):
        out_ref[g, 2 * beams * size :] = coefs


def exchange_kernel(groups, sub_size, sent_ref, got_ref, send_sem, recv_sem, own_sem):
    phonon = lax.axis_index("phonon")
    me = lax.axis_index("beam") * sub_size + lax.axis_index("sub")

    def device(step):
        other = lax.rem(me + step, groups)
        return other, (phonon, lax.div(other, sub_size), lax.rem(other, sub_size))

    barrier = pltpu.get_barrier_semaphore()

    @pl.loop(1, groups)
    def _(step):
        pl.semaphore_signal(
            barrier, inc=1, device_id=device(step)[1], device_id_type=pl.DeviceIdType.MESH
        )

    own = pltpu.make_async_copy(sent_ref.at[me], got_ref.at[me], own_sem)
    own.start()
    pl.semaphore_wait(barrier, groups - 1)

    def copy(step):
        other, place = device(step)
        return pltpu.make_async_remote_copy(
            src_ref=sent_ref.at[other],
            dst_ref=got_ref.at[me],
            send_sem=send_sem.at[step],
            recv_sem=recv_sem.at[step],
            device_id=place,
            device_id_type=pl.DeviceIdType.MESH,
        )

    @pl.loop(1, groups)
    def _(step):
        copy(step).start()

    own.wait()

    @pl.loop(1, groups)
    def _(step):
        copy(step).wait()


def exchange(sent, groups, sub_size):
    vmem = pl.BlockSpec(memory_space=pltpu.VMEM)
    return pl.pallas_call(
        functools.partial(exchange_kernel, groups, sub_size),
        out_shape=jax.ShapeDtypeStruct(sent.shape, sent.dtype),
        in_specs=[vmem],
        out_specs=vmem,
        scratch_shapes=[
            pltpu.SemaphoreType.DMA((groups,)),
            pltpu.SemaphoreType.DMA((groups,)),
            pltpu.SemaphoreType.DMA,
        ],
        compiler_params=pltpu.CompilerParams(
            collective_id=0, has_side_effects=True, vmem_limit_bytes=16 * 1024 * 1024
        ),
    )(sent)


def local_waves(species, cells, profiles, freqs, amplitude, aberration, probes, groups):
    points = profiles.shape[1]
    beams = freqs.shape[1]
    atoms = species.shape[1]
    kept = window_freqs(points)
    window = len(kept)
    grid = np.arange(points)
    coarse = np.arange(NOUT)
    crop = kept[:NOUT]
    fr, fi = table_parts(kept, grid, points, -1.0)
    gr, gi = table_parts(coarse, crop, NOUT, 1.0)
    tables = [
        left_table(fr, fi),
        right_table(fr.T, fi.T),
        left_table(gr, gi),
        right_table(gr.T, gi.T),
        propagator_parts(kept, points),
    ]
    vmem = pl.BlockSpec(memory_space=pltpu.VMEM)
    smem = pl.BlockSpec(memory_space=pltpu.SMEM)
    return pl.pallas_call(
        functools.partial(wave_kernel, beams * groups),
        out_shape=jax.ShapeDtypeStruct((groups, 2 * beams * (NOUT // groups) + 16, NOUT), BF),
        in_specs=[smem] * 3 + [vmem] * (4 + len(tables)),
        out_specs=vmem,
        scratch_shapes=[
            pltpu.VMEM((2 * species.shape[0], points, points), F32),
            pltpu.VMEM((2, points, atoms), BF),
            pltpu.VMEM((2 * points, points), BF),
            pltpu.VMEM((window, 2 * points), BF),
            pltpu.VMEM((2 * window, window), BF),
            pltpu.VMEM((points, 2 * window), BF),
        ],
        compiler_params=pltpu.CompilerParams(vmem_limit_bytes=56 * 1024 * 1024),
    )(freqs, amplitude, aberration, species, cells, profiles, probes, *map(jnp.asarray, tables))


def shards(atom_species, atom_cells, profiles, beam_freqs, amplitude, aberration, probes):
    groups = lax.axis_size("beam") * lax.axis_size("sub")
    beams = beam_freqs.shape[1]
    count = probes.shape[1]
    sent = local_waves(
        atom_species, atom_cells, profiles, beam_freqs, amplitude, aberration, probes, groups
    )
    got = exchange(sent, groups, lax.axis_size("sub"))
    rows = NOUT // groups
    pairs = beams * groups * 2
    coef = got[:, 2 * beams * rows :, :count][:, : 2 * beams].reshape(-1, 2, count)
    coef_re, coef_im = coef[:, 0], coef[:, 1]
    flat = got[:, : 2 * beams * rows].reshape(pairs, rows * NOUT)
    left_re = jnp.stack([coef_re, -coef_im], axis=1).reshape(pairs, count)
    left_im = jnp.stack([coef_im, coef_re], axis=1).reshape(pairs, count)
    over = (((0,), (0,)), ((), ()))
    psi_re = lax.dot_general(left_re, flat, over, preferred_element_type=F32)
    psi_im = lax.dot_general(left_im, flat, over, preferred_element_type=F32)
    return (psi_re * psi_re + psi_im * psi_im).reshape(count, rows, NOUT)


def solution(mesh):
    return jax.shard_map(
        shards,
        mesh=mesh,
        in_specs=(
            P("phonon", None),
            P(None, "phonon", None),
            P(),
            P(None, ("beam", "sub")),
            P(("beam", "sub")),
            P(("beam", "sub")),
            P(),
        ),
        out_specs=P("phonon", ("beam", "sub"), None),
        check_vma=False,
    )
```

```python
import functools
import math

import jax
import jax.numpy as jnp
import ml_dtypes
import numpy as np
from jax import lax
from jax.experimental import pallas as pl
from jax.experimental.pallas import tpu as pltpu
from jax.sharding import PartitionSpec as P

NOUT = 256
LOW = 64
BF = jnp.bfloat16
F32 = jnp.float32


def fit_turn_polys():
    nodes = np.cos(np.pi * (np.arange(400) + 0.5) / 400)
    squares = (nodes + 1.0) * 0.125
    turns = np.sqrt(squares)
    cosine = np.polynomial.chebyshev.Chebyshev.fit(
        squares, np.cos(2 * np.pi * turns), 6, domain=[0, 0.25]
    )
    sine = np.polynomial.chebyshev.Chebyshev.fit(
        squares, np.sin(2 * np.pi * turns) / turns, 6, domain=[0, 0.25]
    )
    to_list = lambda fit: [float(c) for c in fit.convert(kind=np.polynomial.Polynomial).coef]
    return to_list(cosine), to_list(sine)


COS_POLY, SIN_POLY = fit_turn_polys()


def cos_sin_turns(turns):
    rest = turns - jnp.round(turns)
    square = rest * rest
    cosine = jnp.full_like(square, COS_POLY[-1])
    for c in COS_POLY[-2::-1]:
        cosine = cosine * square + c
    sine = jnp.full_like(square, SIN_POLY[-1])
    for c in SIN_POLY[-2::-1]:
        sine = sine * square + c
    return cosine, sine * rest


def window_freqs(points):
    half = NOUT // 2
    reach = math.isqrt((points * points - 1) // 9)
    side = max(reach + 1, half)
    side = min(-(-side // 64) * 64, points // 2)
    return np.concatenate(
        [np.arange(-half, half), np.arange(half, side), np.arange(-side, -half)]
    ).astype(np.int64)


def table_parts(rows, cols, modulus, sign):
    angle = sign * 2.0 * np.pi / modulus * np.mod(rows[:, None] * cols[None, :], modulus)
    return np.cos(angle), np.sin(angle)


def left_table(real, imag):
    return np.block([[real, -imag], [imag, real]]).astype(ml_dtypes.bfloat16)


def right_table(real, imag):
    return np.block([[real, imag], [-imag, real]]).astype(ml_dtypes.bfloat16)


def propagator_parts(freqs, points):
    q = freqs[:, None] ** 2 + freqs[None, :] ** 2
    angle = -np.pi / points * np.mod(q, 2 * points)
    window = np.where(9 * q < points * points, 1.0 / (points * points), 0.0)
    return np.stack([np.cos(angle) * window, np.sin(angle) * window]).astype(np.float32)


def dot(a, b):
    return jnp.dot(a, b, preferred_element_type=F32)


def wave_kernel(
    total_beams,
    freqs_ref,
    amp_ref,
    aber_ref,
    species_ref,
    cells_ref,
    prof_ref,
    probes_ref,
    lf_ref,
    rf_ref,
    lgc_ref,
    rgc_ref,
    pf_ref,
    out_ref,
    field_ref,
    rows_ref,
    tall_ref,
    wide_ref,
    tall_c,
    wide_c,
):
    kinds, points = prof_ref.shape
    slices, atoms = species_ref.shape
    beams = freqs_ref.shape[1]
    groups = out_ref.shape[0]
    size = NOUT // groups
    window = pf_ref.shape[1]

    stacked = []
    for s in range(kinds):
        row = jnp.broadcast_to(prof_ref[s : s + 1, :].astype(F32), (LOW, points))
        stacked.append(pltpu.roll(row, 0, 1, stride=1, stride_axis=0))
    tab = jnp.transpose(jnp.concatenate(stacked, axis=0)).astype(BF)

    scale = 1.5 / math.sqrt(atoms) / (2.0 * math.pi)
    chunk = min(512, atoms)
    slot = lax.broadcasted_iota(jnp.int32, (kinds * LOW, chunk), 0)
    for layer in range(slices):
        for axis in range(2):
            for first in range(0, atoms, chunk):
                here = slice(first, first + chunk)
                cell = cells_ref[axis, layer : layer + 1, here]
                key = species_ref[layer : layer + 1, here] * LOW + jnp.bitwise_and(cell, LOW - 1)
                picked = (slot == key).astype(F32).astype(BF)
                rows = dot(tab, picked).astype(BF)
                amount = LOW
                while amount < points:
                    moved = jnp.concatenate([rows[points - amount :], rows[: points - amount]], 0)
                    bit = (jnp.bitwise_and(cell, amount) != 0).astype(F32).astype(BF)
                    rows = jnp.where(jnp.broadcast_to(bit, rows.shape) > 0.5, moved, rows)
                    amount *= 2
                rows_ref[axis, :, here] = rows
        field = lax.dot_general(
            rows_ref[0], rows_ref[1], (((1,), (1,)), ((), ())), preferred_element_type=F32
        )
        cosine, sine = cos_sin_turns(field * scale)
        field_ref[2 * layer] = cosine
        field_ref[2 * layer + 1] = sine

    down = lax.broadcasted_iota(jnp.int32, (points, 1), 0)
    along = lax.broadcasted_iota(jnp.int32, (1, points), 1)
    coef_rows = []
    for b in range(beams):
        fx, fy = freqs_ref[0, b], freqs_ref[1, b]
        col_re, col_im = cos_sin_turns(
            jnp.bitwise_and(down * fx, points - 1).astype(F32) * (1.0 / points)
        )
        row_re, row_im = cos_sin_turns(
            jnp.bitwise_and(along * fy, points - 1).astype(F32) * (1.0 / points)
        )
        wave_re = col_re * row_re - col_im * row_im
        wave_im = col_re * row_im + col_im * row_re
        for layer in range(slices):
            tr, ti = field_ref[2 * layer], field_ref[2 * layer + 1]
            tall_ref[:points] = (wave_re * tr - wave_im * ti).astype(BF)
            tall_ref[points:] = (wave_re * ti + wave_im * tr).astype(BF)
            last = layer == slices - 1
            n = NOUT if last else window
            lg, rg = (lgc_ref, rgc_ref) if last else (rf_ref, lf_ref)
            width = rg.shape[1] // 2
            wide_ref[:n, :points] = dot(lf_ref[:n], tall_ref[...]).astype(BF)
            wide_ref[:n, points:] = dot(lf_ref[window : window + n], tall_ref[...]).astype(BF)
            half = wide_ref[:n]
            sr = dot(half, rf_ref[:, :n])
            si = dot(half, rf_ref[:, window : window + n])
            pr, pi = pf_ref[0, :n, :n], pf_ref[1, :n, :n]
            tall_c[:n, :n] = (sr * pr - si * pi).astype(BF)
            tall_c[n : 2 * n, :n] = (sr * pi + si * pr).astype(BF)
            shaped = tall_c[: 2 * n, :n]
            wide_c[:width, :n] = dot(lg[:width], shaped).astype(BF)
            wide_c[:width, n : 2 * n] = dot(lg[width:], shaped).astype(BF)
            back = wide_c[:width, : 2 * n]
            wave_re = dot(back, rg[:, :width])
            wave_im = dot(back, rg[:, width:])
        for part, wave in enumerate((wave_re, wave_im)):
            start = (2 * b + part) * size
            if size % 16 == 0:
                for g in range(groups):
                    out_ref[g, start : start + size] = wave[g * size : (g + 1) * size].astype(BF)
            else:
                blocks = wave.reshape(groups, size, NOUT).astype(BF)
                out_ref[:, start : start + size] = blocks
        place = probes_ref[0:1, :] * fx + probes_ref[1:2, :] * fy
        turns = jnp.bitwise_and(place, NOUT - 1).astype(F32) * (1.0 / NOUT)
        cosine, sine = cos_sin_turns(turns + aber_ref[b] * (0.5 / math.pi))
        weight = amp_ref[b] * (1.0 / math.sqrt(total_beams))
        coef_rows += [weight * cosine, -(weight * sine)]
    count = probes_ref.shape[1]
    coefs = jnp.concatenate(coef_rows, axis=0)
    coefs = jnp.pad(coefs, ((0, 16 - 2 * beams), (0, NOUT - count))).astype(BF)
    for g in range(groups):
        out_ref[g, 2 * beams * size :] = coefs


def exchange_kernel(groups, sub_size, sent_ref, got_ref, send_sem, recv_sem, own_sem):
    phonon = lax.axis_index("phonon")
    me = lax.axis_index("beam") * sub_size + lax.axis_index("sub")

    def device(step):
        other = lax.rem(me + step, groups)
        return other, (phonon, lax.div(other, sub_size), lax.rem(other, sub_size))

    barrier = pltpu.get_barrier_semaphore()

    @pl.loop(1, groups)
    def _(step):
        pl.semaphore_signal(
            barrier, inc=1, device_id=device(step)[1], device_id_type=pl.DeviceIdType.MESH
        )

    own = pltpu.make_async_copy(sent_ref.at[me], got_ref.at[me], own_sem)
    own.start()
    pl.semaphore_wait(barrier, groups - 1)

    def copy(step):
        other, place = device(step)
        return pltpu.make_async_remote_copy(
            src_ref=sent_ref.at[other],
            dst_ref=got_ref.at[me],
            send_sem=send_sem.at[step],
            recv_sem=recv_sem.at[step],
            device_id=place,
            device_id_type=pl.DeviceIdType.MESH,
        )

    @pl.loop(1, groups)
    def _(step):
        copy(step).start()

    own.wait()

    @pl.loop(1, groups)
    def _(step):
        copy(step).wait()


def exchange(sent, groups, sub_size):
    place = pl.BlockSpec(memory_space=pl.ANY)
    return pl.pallas_call(
        functools.partial(exchange_kernel, groups, sub_size),
        out_shape=jax.ShapeDtypeStruct(sent.shape, sent.dtype),
        in_specs=[place],
        out_specs=place,
        scratch_shapes=[
            pltpu.SemaphoreType.DMA((groups,)),
            pltpu.SemaphoreType.DMA((groups,)),
            pltpu.SemaphoreType.DMA,
        ],
        compiler_params=pltpu.CompilerParams(
            collective_id=0, has_side_effects=True, vmem_limit_bytes=16 * 1024 * 1024
        ),
    )(sent)


def local_waves(species, cells, profiles, freqs, amplitude, aberration, probes, groups):
    points = profiles.shape[1]
    beams = freqs.shape[1]
    atoms = species.shape[1]
    kept = window_freqs(points)
    window = len(kept)
    grid = np.arange(points)
    coarse = np.arange(NOUT)
    crop = kept[:NOUT]
    fr, fi = table_parts(kept, grid, points, -1.0)
    gr, gi = table_parts(coarse, crop, NOUT, 1.0)
    tables = [
        left_table(fr, fi),
        right_table(fr.T, fi.T),
        left_table(gr, gi),
        right_table(gr.T, gi.T),
        propagator_parts(kept, points),
    ]
    vmem = pl.BlockSpec(memory_space=pltpu.VMEM)
    smem = pl.BlockSpec(memory_space=pltpu.SMEM)
    return pl.pallas_call(
        functools.partial(wave_kernel, beams * groups),
        out_shape=jax.ShapeDtypeStruct((groups, 2 * beams * (NOUT // groups) + 16, NOUT), BF),
        in_specs=[smem] * 3 + [vmem] * (4 + len(tables)),
        out_specs=vmem,
        scratch_shapes=[
            pltpu.VMEM((2 * species.shape[0], points, points), F32),
            pltpu.VMEM((2, points, atoms), BF),
            pltpu.VMEM((2 * points, points), BF),
            pltpu.VMEM((window, 2 * points), BF),
            pltpu.VMEM((2 * window, window), BF),
            pltpu.VMEM((points, 2 * window), BF),
        ],
        compiler_params=pltpu.CompilerParams(vmem_limit_bytes=56 * 1024 * 1024),
    )(freqs, amplitude, aberration, species, cells, profiles, probes, *map(jnp.asarray, tables))


def shards(atom_species, atom_cells, profiles, beam_freqs, amplitude, aberration, probes):
    groups = lax.axis_size("beam") * lax.axis_size("sub")
    beams = beam_freqs.shape[1]
    count = probes.shape[1]
    sent = local_waves(
        atom_species, atom_cells, profiles, beam_freqs, amplitude, aberration, probes, groups
    )
    got = exchange(sent, groups, lax.axis_size("sub"))
    rows = NOUT // groups
    pairs = beams * groups * 2
    coef = got[:, 2 * beams * rows :, :count][:, : 2 * beams].reshape(-1, 2, count)
    coef_re, coef_im = coef[:, 0], coef[:, 1]
    flat = got[:, : 2 * beams * rows].reshape(pairs, rows * NOUT)
    left_re = jnp.stack([coef_re, -coef_im], axis=1).reshape(pairs, count)
    left_im = jnp.stack([coef_im, coef_re], axis=1).reshape(pairs, count)
    over = (((0,), (0,)), ((), ()))
    psi_re = lax.dot_general(left_re, flat, over, preferred_element_type=F32)
    psi_im = lax.dot_general(left_im, flat, over, preferred_element_type=F32)
    return (psi_re * psi_re + psi_im * psi_im).reshape(count, rows, NOUT)


def solution(mesh):
    return jax.shard_map(
        shards,
        mesh=mesh,
        in_specs=(
            P("phonon", None),
            P(None, "phonon", None),
            P(),
            P(None, ("beam", "sub")),
            P(("beam", "sub")),
            P(("beam", "sub")),
            P(),
        ),
        out_specs=P("phonon", ("beam", "sub"), None),
        check_vma=False,
    )
```

```python
import functools
import math

import jax
import jax.numpy as jnp
import ml_dtypes
import numpy as np
from jax import lax
from jax.experimental import pallas as pl
from jax.experimental.pallas import tpu as pltpu
from jax.sharding import PartitionSpec as P

NOUT = 256
LOW = 64
BF = jnp.bfloat16
F32 = jnp.float32


def fit_turn_polys():
    nodes = np.cos(np.pi * (np.arange(400) + 0.5) / 400)
    squares = (nodes + 1.0) * 0.125
    turns = np.sqrt(squares)
    cosine = np.polynomial.chebyshev.Chebyshev.fit(
        squares, np.cos(2 * np.pi * turns), 6, domain=[0, 0.25]
    )
    sine = np.polynomial.chebyshev.Chebyshev.fit(
        squares, np.sin(2 * np.pi * turns) / turns, 6, domain=[0, 0.25]
    )
    to_list = lambda fit: [float(c) for c in fit.convert(kind=np.polynomial.Polynomial).coef]
    return to_list(cosine), to_list(sine)


COS_POLY, SIN_POLY = fit_turn_polys()


def cos_sin_turns(turns):
    rest = turns - jnp.round(turns)
    square = rest * rest
    cosine = jnp.full_like(square, COS_POLY[-1])
    for c in COS_POLY[-2::-1]:
        cosine = cosine * square + c
    sine = jnp.full_like(square, SIN_POLY[-1])
    for c in SIN_POLY[-2::-1]:
        sine = sine * square + c
    return cosine, sine * rest


def window_freqs(points):
    half = NOUT // 2
    reach = math.isqrt((points * points - 1) // 9)
    side = max(reach + 1, half)
    side = min(-(-side // 64) * 64, points // 2)
    return np.concatenate(
        [np.arange(-half, half), np.arange(half, side), np.arange(-side, -half)]
    ).astype(np.int64)


def table_parts(rows, cols, modulus, sign):
    angle = sign * 2.0 * np.pi / modulus * np.mod(rows[:, None] * cols[None, :], modulus)
    return np.cos(angle), np.sin(angle)


def left_table(real, imag):
    return np.block([[real, -imag], [imag, real]]).astype(ml_dtypes.bfloat16)


def right_table(real, imag):
    return np.block([[real, imag], [-imag, real]]).astype(ml_dtypes.bfloat16)


def propagator_parts(freqs, points):
    q = freqs[:, None] ** 2 + freqs[None, :] ** 2
    angle = -np.pi / points * np.mod(q, 2 * points)
    window = np.where(9 * q < points * points, 1.0 / (points * points), 0.0)
    return np.stack([np.cos(angle) * window, np.sin(angle) * window]).astype(np.float32)


def dot(a, b):
    return jnp.dot(a, b, preferred_element_type=F32)


def wave_kernel(
    total_beams,
    freqs_ref,
    amp_ref,
    aber_ref,
    species_ref,
    cells_ref,
    prof_ref,
    probes_ref,
    lf_ref,
    rf_ref,
    lgc_ref,
    rgc_ref,
    pf_ref,
    out_ref,
    field_ref,
    rows_ref,
    tall_ref,
    wide_ref,
    tall_c,
    wide_c,
):
    kinds, points = prof_ref.shape
    slices, atoms = species_ref.shape
    beams = freqs_ref.shape[1]
    groups = out_ref.shape[0]
    size = NOUT // groups
    window = pf_ref.shape[1]

    stacked = []
    for s in range(kinds):
        row = jnp.broadcast_to(prof_ref[s : s + 1, :].astype(F32), (LOW, points))
        stacked.append(pltpu.roll(row, 0, 1, stride=1, stride_axis=0))
    tab = jnp.transpose(jnp.concatenate(stacked, axis=0)).astype(BF)

    scale = 1.5 / math.sqrt(atoms) / (2.0 * math.pi)
    chunk = min(512, atoms)
    slot = lax.broadcasted_iota(jnp.int32, (kinds * LOW, chunk), 0)
    for layer in range(slices):
        for axis in range(2):
            for first in range(0, atoms, chunk):
                here = slice(first, first + chunk)
                cell = cells_ref[axis, layer : layer + 1, here]
                key = species_ref[layer : layer + 1, here] * LOW + jnp.bitwise_and(cell, LOW - 1)
                picked = (slot == key).astype(F32).astype(BF)
                rows = dot(tab, picked).astype(BF)
                amount = LOW
                while amount < points:
                    moved = jnp.concatenate([rows[points - amount :], rows[: points - amount]], 0)
                    bit = (jnp.bitwise_and(cell, amount) != 0).astype(F32).astype(BF)
                    rows = jnp.where(jnp.broadcast_to(bit, rows.shape) > 0.5, moved, rows)
                    amount *= 2
                rows_ref[axis, :, here] = rows
        field = lax.dot_general(
            rows_ref[0], rows_ref[1], (((1,), (1,)), ((), ())), preferred_element_type=F32
        )
        cosine, sine = cos_sin_turns(field * scale)
        field_ref[2 * layer] = cosine
        field_ref[2 * layer + 1] = sine

    down = lax.broadcasted_iota(jnp.int32, (points, 1), 0)
    along = lax.broadcasted_iota(jnp.int32, (1, points), 1)
    coef_rows = []
    for b in range(beams):
        fx, fy = freqs_ref[0, b], freqs_ref[1, b]
        col_re, col_im = cos_sin_turns(
            jnp.bitwise_and(down * fx, points - 1).astype(F32) * (1.0 / points)
        )
        row_re, row_im = cos_sin_turns(
            jnp.bitwise_and(along * fy, points - 1).astype(F32) * (1.0 / points)
        )
        wave_re = col_re * row_re - col_im * row_im
        wave_im = col_re * row_im + col_im * row_re
        for layer in range(slices):
            tr, ti = field_ref[2 * layer], field_ref[2 * layer + 1]
            tall_ref[:points] = (wave_re * tr - wave_im * ti).astype(BF)
            tall_ref[points:] = (wave_re * ti + wave_im * tr).astype(BF)
            last = layer == slices - 1
            n = NOUT if last else window
            lg, rg = (lgc_ref, rgc_ref) if last else (rf_ref, lf_ref)
            width = rg.shape[1] // 2
            wide_ref[:n, :points] = dot(lf_ref[:n], tall_ref[...]).astype(BF)
            wide_ref[:n, points:] = dot(lf_ref[window : window + n], tall_ref[...]).astype(BF)
            half = wide_ref[:n]
            sr = dot(half, rf_ref[:, :n])
            si = dot(half, rf_ref[:, window : window + n])
            pr, pi = pf_ref[0, :n, :n], pf_ref[1, :n, :n]
            tall_c[:n, :n] = (sr * pr - si * pi).astype(BF)
            tall_c[n : 2 * n, :n] = (sr * pi + si * pr).astype(BF)
            shaped = tall_c[: 2 * n, :n]
            wide_c[:width, :n] = dot(lg[:width], shaped).astype(BF)
            wide_c[:width, n : 2 * n] = dot(lg[width:], shaped).astype(BF)
            back = wide_c[:width, : 2 * n]
            wave_re = dot(back, rg[:, :width])
            wave_im = dot(back, rg[:, width:])
        for part, wave in enumerate((wave_re, wave_im)):
            start = (2 * b + part) * size
            if size % 16 == 0:
                for g in range(groups):
                    out_ref[g, start : start + size] = wave[g * size : (g + 1) * size].astype(BF)
            else:
                blocks = wave.reshape(groups, size, NOUT).astype(BF)
                out_ref[:, start : start + size] = blocks
        place = probes_ref[0:1, :] * fx + probes_ref[1:2, :] * fy
        turns = jnp.bitwise_and(place, NOUT - 1).astype(F32) * (1.0 / NOUT)
        cosine, sine = cos_sin_turns(turns + aber_ref[b] * (0.5 / math.pi))
        weight = amp_ref[b] * (1.0 / math.sqrt(total_beams))
        coef_rows += [weight * cosine, -(weight * sine)]
    count = probes_ref.shape[1]
    coefs = jnp.concatenate(coef_rows, axis=0)
    coefs = jnp.pad(coefs, ((0, 16 - 2 * beams), (0, NOUT - count))).astype(BF)
    for g in range(groups):
        out_ref[g, 2 * beams * size :] = coefs


def exchange_kernel(groups, sub_size, main, lanes, sent_ref, got_ref, send_sem, recv_sem, own_sem):
    phonon = lax.axis_index("phonon")
    me = lax.axis_index("beam") * sub_size + lax.axis_index("sub")

    def device(step):
        other = lax.rem(me + step, groups)
        return other, (phonon, lax.div(other, sub_size), lax.rem(other, sub_size))

    barrier = pltpu.get_barrier_semaphore()

    @pl.loop(1, groups)
    def _(step):
        pl.semaphore_signal(
            barrier, inc=1, device_id=device(step)[1], device_id_type=pl.DeviceIdType.MESH
        )

    own = pltpu.make_async_copy(sent_ref.at[me], got_ref.at[me], own_sem)
    own.start()
    pl.semaphore_wait(barrier, groups - 1)

    def copies(turn):
        step = lax.rem(turn - 1 + groups // 4, groups - 1) + 1
        other, place = device(step)
        pieces = ((pl.ds(0, main), pl.ds(0, NOUT)), (pl.ds(main, 16), pl.ds(0, lanes)))
        return [
            pltpu.make_async_remote_copy(
                src_ref=sent_ref.at[other, rows, cols],
                dst_ref=got_ref.at[me, rows, cols],
                send_sem=send_sem.at[k, step],
                recv_sem=recv_sem.at[k, step],
                device_id=place,
                device_id_type=pl.DeviceIdType.MESH,
            )
            for k, (rows, cols) in enumerate(pieces)
        ]

    @pl.loop(1, groups)
    def _(turn):
        for copy in copies(turn):
            copy.start()

    own.wait()

    @pl.loop(1, groups)
    def _(turn):
        for copy in copies(turn):
            copy.wait()


def exchange(sent, groups, sub_size, count):
    lanes = min(-(-count // 128) * 128, NOUT)
    place = pl.BlockSpec(memory_space=pl.ANY)
    return pl.pallas_call(
        functools.partial(exchange_kernel, groups, sub_size, sent.shape[1] - 16, lanes),
        out_shape=jax.ShapeDtypeStruct(sent.shape, sent.dtype),
        in_specs=[place],
        out_specs=place,
        scratch_shapes=[
            pltpu.SemaphoreType.DMA((2, groups)),
            pltpu.SemaphoreType.DMA((2, groups)),
            pltpu.SemaphoreType.DMA,
        ],
        compiler_params=pltpu.CompilerParams(
            collective_id=0, has_side_effects=True, vmem_limit_bytes=16 * 1024 * 1024
        ),
    )(sent)


def local_waves(species, cells, profiles, freqs, amplitude, aberration, probes, groups):
    points = profiles.shape[1]
    beams = freqs.shape[1]
    atoms = species.shape[1]
    kept = window_freqs(points)
    window = len(kept)
    grid = np.arange(points)
    coarse = np.arange(NOUT)
    crop = kept[:NOUT]
    fr, fi = table_parts(kept, grid, points, -1.0)
    gr, gi = table_parts(coarse, crop, NOUT, 1.0)
    tables = [
        left_table(fr, fi),
        right_table(fr.T, fi.T),
        left_table(gr, gi),
        right_table(gr.T, gi.T),
        propagator_parts(kept, points),
    ]
    vmem = pl.BlockSpec(memory_space=pltpu.VMEM)
    smem = pl.BlockSpec(memory_space=pltpu.SMEM)
    return pl.pallas_call(
        functools.partial(wave_kernel, beams * groups),
        out_shape=jax.ShapeDtypeStruct((groups, 2 * beams * (NOUT // groups) + 16, NOUT), BF),
        in_specs=[smem] * 3 + [vmem] * (4 + len(tables)),
        out_specs=vmem,
        scratch_shapes=[
            pltpu.VMEM((2 * species.shape[0], points, points), F32),
            pltpu.VMEM((2, points, atoms), BF),
            pltpu.VMEM((2 * points, points), BF),
            pltpu.VMEM((window, 2 * points), BF),
            pltpu.VMEM((2 * window, window), BF),
            pltpu.VMEM((points, 2 * window), BF),
        ],
        compiler_params=pltpu.CompilerParams(vmem_limit_bytes=56 * 1024 * 1024),
    )(freqs, amplitude, aberration, species, cells, profiles, probes, *map(jnp.asarray, tables))


def shards(atom_species, atom_cells, profiles, beam_freqs, amplitude, aberration, probes):
    groups = lax.axis_size("beam") * lax.axis_size("sub")
    beams = beam_freqs.shape[1]
    count = probes.shape[1]
    sent = local_waves(
        atom_species, atom_cells, profiles, beam_freqs, amplitude, aberration, probes, groups
    )
    got = exchange(sent, groups, lax.axis_size("sub"), count)
    rows = NOUT // groups
    pairs = beams * groups * 2
    coef = got[:, 2 * beams * rows :, :count][:, : 2 * beams].reshape(-1, 2, count)
    coef_re, coef_im = coef[:, 0], coef[:, 1]
    flat = got[:, : 2 * beams * rows].reshape(pairs, rows * NOUT)
    left_re = jnp.stack([coef_re, -coef_im], axis=1).reshape(pairs, count)
    left_im = jnp.stack([coef_im, coef_re], axis=1).reshape(pairs, count)
    over = (((0,), (0,)), ((), ()))
    psi_re = lax.dot_general(left_re, flat, over, preferred_element_type=F32)
    psi_im = lax.dot_general(left_im, flat, over, preferred_element_type=F32)
    return (psi_re * psi_re + psi_im * psi_im).reshape(count, rows, NOUT)


def solution(mesh):
    return jax.shard_map(
        shards,
        mesh=mesh,
        in_specs=(
            P("phonon", None),
            P(None, "phonon", None),
            P(),
            P(None, ("beam", "sub")),
            P(("beam", "sub")),
            P(("beam", "sub")),
            P(),
        ),
        out_specs=P("phonon", ("beam", "sub"), None),
        check_vma=False,
    )
```
